256 devices in a mesh: tm: 8 (over z_lo, core), pix: 32 (over x, y, z_hi).
Axes of the slice: x: 4, y: 4, z: 8 (z_hi: 2, z_lo: 4; z = z_hi * 4 + z_lo), core: 2. Of those that a mesh axis runs over, the one named last changes fastest.
Arguments:
- frames: float32 [2048, 32768], P('tm', 'pix'), may hold values from -6 to 6
- ann_rows: int32 [256], P('pix'), may hold values from 0 to 3, as said below
- start_bases: float32 [4, 2048, 256], P(None, ('tm', 'pix')), may hold values from -0.125 to 0.125
Outputs:
- cleaned: float32 [2048, 32768], P('tm', 'pix')
The draws below stay inside these ranges and needn't reach their ends.
Inputs may be any that keep to these rules, and one draw needn't show every extreme that they name: `ann_rows`: annulus numbers never fall along the rows; every annulus holds at least 32 rows, and one holds exactly that many.
All inputs are finite; a program needn't handle non-finite values.
Results may differ from the reference program's by a relative error of at most 0.0003.
Values sent between devices are 32-bit elements; how exact they have to be, the bound alone decides.
A program may use at most 64 MiB of HBM per device.

```python
import jax
import jax.numpy as jnp
from jax import lax

F = 2048
K = 256
ANN = 4
ITERS = 2
P_SIZE = 32768
ROWS = 256


def draw_ann_rows(key, part):
    key = jax.random.fold_in(key, 11)
    minimum_rows = ROWS // (2 * ANN)
    spare_rows = ROWS - ANN * minimum_rows
    key_lean, key_left, key_right = jax.random.split(key, 3)
    leanest = jax.random.randint(key_lean, (), 0, ANN)
    chosen = jnp.minimum(jax.random.randint(key_left, (spare_rows,), 0, ANN - 1), jax.random.randint(key_right, (spare_rows,), 0, ANN - 1))
    chosen = chosen + (chosen >= leanest).astype(jnp.int32)
    annulus_ids = jnp.arange(ANN, dtype=jnp.int32)
    row_counts = minimum_rows + jnp.sum((chosen[None, :] == annulus_ids[:, None]).astype(jnp.int32), axis=1)
    upper_edges = jnp.cumsum(row_counts)
    row_index = jnp.arange(ROWS, dtype=jnp.int32)
    return jnp.sum((row_index[:, None] >= upper_edges[None, :]).astype(jnp.int32), axis=1).astype(jnp.int32)


def steps_of(own_key, dims, cuts, smallest, high):
    def one(dim, shards_of):
        draws = jax.random.uniform(jax.random.fold_in(jax.random.fold_in(own_key, 6), dim), (shards_of,), jnp.float32, smallest / len(cuts), high / len(cuts))
        return jnp.repeat(jnp.exp(draws), dims[dim] // shards_of).reshape((-1,) + (1,) * (len(dims) - dim - 1))

    factor_of = one(*cuts[0])
    for cut in cuts[1:]:
        factor_of = factor_of * one(*cut)
    return factor_of


def scatter_about(stream_key, dims, width, bound, shards=(), kind=jnp.bfloat16):
    array = jax.random.normal(stream_key, dims, jnp.float32) * width
    if len(shards) > 0:
        array = steps_of(stream_key, dims, shards, -0.22, 0.18) * array
    return jnp.clip(array, min=-bound, max=bound).astype(kind)


def setup_inputs(seed: int = 0) -> dict:
    splits = jax.random.split(jax.random.key(seed), 4)
    frames = scatter_about(splits[0], (F, P_SIZE), 1.0, 6.0, ((0, 8), (1, 32)), jnp.float32)
    ann_rows = draw_ann_rows(jax.random.fold_in(splits[3], 71), 0)
    start_bases = scatter_about(splits[2], (ANN, F, K), F ** -0.5, 0.125, ((1, 256),), jnp.float32)
    return dict(frames=frames, ann_rows=ann_rows, start_bases=start_bases)


def orthonormal(product):
    squares = jnp.einsum('aik,ail->akl', product, product, precision=lax.Precision.HIGHEST)
    factor = jnp.linalg.cholesky(squares)
    solved = jax.scipy.linalg.solve_triangular(factor, jnp.swapaxes(product, 1, 2), lower=True)
    return jnp.swapaxes(solved, 1, 2)

def reference(frames, ann_rows, start_bases):
    highest = lax.Precision.HIGHEST
    pixel_annulus = jnp.repeat(ann_rows, 128)
    annulus_ids = jnp.arange(ANN, dtype=jnp.int32)
    annulus_mask = (pixel_annulus[None, :] == annulus_ids[:, None]).astype(jnp.float32)
    gram_list = []
    for annulus in range(ANN):
        masked = frames * annulus_mask[annulus][None, :]
        gram_list.append(jnp.einsum('fp,gp->fg', masked, masked, precision=highest))
    gram_all = jnp.stack(gram_list)
    current = start_bases
    for sweep in range(ITERS):
        product = jnp.einsum('afg,agk->afk', gram_all, current, precision=highest)
        current = orthonormal(product)
    cleaned = frames
    for annulus in range(ANN):
        masked = frames * annulus_mask[annulus][None, :]
        coefficients = jnp.einsum('fk,fp->kp', current[annulus], masked, precision=highest)
        cleaned = cleaned - jnp.dot(current[annulus].astype(jnp.float32), coefficients.astype(jnp.float32), precision=highest, preferred_element_type=jnp.float32)
    return cleaned
```

```python
import jax
import jax.numpy as jnp
from jax import lax
from jax.experimental import pallas as pl
from jax.experimental.pallas import tpu as pltpu
from jax.sharding import PartitionSpec as P

MESH = pl.DeviceIdType.MESH
F32 = jnp.float32
BF16 = jnp.bfloat16
HIGHEST = lax.Precision.HIGHEST
ANN = 4
K = 256
NPL = 16
NN = (((1,), (0,)), ((), ()))
NT = (((1,), (1,)), ((), ()))


def dot(a, b, dims=NN):
    return lax.dot_general(a, b, dims, preferred_element_type=F32)


def dot_full(a, b, dims=NN):
    return lax.dot_general(a, b, dims, precision=HIGHEST, preferred_element_type=F32)


def split(a):
    high = a.astype(BF16)
    return high, (a - high.astype(F32)).astype(BF16)


def dot3(ah, al, bh, bl, dims=NN):
    return dot(ah, bh, dims) + (dot(ah, bl, dims) + dot(al, bh, dims))


def leaf(a):
    n = 128
    groups = n // 8
    sub = lax.broadcasted_iota(jnp.int32, (8, n), 0)
    lane = lax.broadcasted_iota(jnp.int32, (8, n), 1)
    left = [a[8 * g : 8 * g + 8, :] for g in range(groups)]
    right = [jnp.where(lane == sub + 8 * g, 1.0, 0.0).astype(F32) for g in range(groups)]
    for k in range(n):
        g0, k0 = k // 8, k % 8
        columns = [jnp.broadcast_to(left[g][:, k : k + 1], (8, n)) for g in range(g0, groups)]
        pivot = columns[0][k0 : k0 + 1, :]
        inverse = 1.0 / pivot
        row_left = left[g0][k0 : k0 + 1, :] * inverse
        row_right = right[g0][k0 : k0 + 1, :] * inverse
        scale = lax.rsqrt(pivot)
        for g in range(g0, groups):
            column = columns[g - g0]
            if g == g0:
                column = jnp.where(sub > k0, column, 0.0)
            left[g] = left[g] - column * row_left
            right[g] = right[g] - column * row_right
        right[g0] = jnp.where(sub == k0, right[g0] * scale, right[g0])
    return jnp.concatenate(right, 0)


def inverse_factor(s_ref, out_ref):
    first = leaf(s_ref[0:128, 0:128])
    out_ref[0:128, 0:128] = first
    out_ref[0:128, 128:256] = jnp.zeros((128, 128), F32)
    lower = dot_full(s_ref[128:256, 0:128], first, NT)
    second = leaf(s_ref[128:256, 128:256] - dot_full(lower, lower, NT))
    out_ref[128:256, 128:256] = second
    out_ref[128:256, 0:128] = -dot_full(second, dot_full(lower, out_ref[0:128, 0:128]))


def kernel(
    frames, ids, base, out,
    xw, xh, xl, xth, xtl, bs, bh, bl, zb,
    own, erecv, mrecv, tot, ymh, yml,
    pbuf, prec, rsend, rrecv, st, zrecv, gbuf, idtile, idall,
    smat, linv, y3, ot,
    core_send, core_recv, plane_send, plane_recv, zsend, zrec, line_send, line_recv,
):
    t, p = lax.axis_index("tm"), lax.axis_index("pix")
    c, zl = lax.rem(t, 2), t // 2
    q, zh = p // 2, lax.rem(p, 2)
    is_mid = jnp.logical_or(zl == 1, zl == 2)
    is_end = jnp.logical_or(zl == 0, zl == 3)
    other = {"tm": t + 1 - 2 * c, "pix": p}
    across = {"tm": t, "pix": 2 * q + 1 - zh}
    pair = {"tm": 2 * (zl + 1 - 2 * lax.rem(zl, 2)) + c, "pix": p}
    middle = {"tm": 2 * (3 - zl) + c, "pix": p}

    def peer(d):
        return {"tm": t, "pix": 2 * d + zh}

    def remote(src, dst, send, recv, device):
        return pltpu.make_async_remote_copy(
            src_ref=src, dst_ref=dst, send_sem=send, recv_sem=recv, device_id=device, device_id_type=MESH
        )

    def greet(device):
        pl.semaphore_signal(barrier, inc=1, device_id=device, device_id_type=MESH)

    def each_peer(body):
        def step(d, _):
            body(lax.rem(q + d, NPL))
            return 0

        lax.fori_loop(1, NPL, step, 0)

    barrier = pltpu.get_barrier_semaphore()
    greet(other)
    greet(across)
    greet(pair)
    each_peer(lambda d: greet(peer(d)))

    @pl.when(is_mid)
    def _():
        greet(middle)

    first_id, last_id = ids[0], ids[7]
    idtile[0:1, :] = jnp.full((1, K), first_id, jnp.int32)
    idtile[1:2, :] = jnp.full((1, K), last_id, jnp.int32)
    idtile[2:8, :] = jnp.zeros((6, K), jnp.int32)
    idall[q] = idtile[...]
    pl.semaphore_wait(barrier, jnp.where(is_mid, 19, 18))

    def x_copy(side):
        return remote(
            frames.at[:, pl.ds(pl.multiple_of((1 - c) * 512, 128), 512)],
            xw.at[pl.ds(pl.multiple_of(side * 256, 256), 256), :],
            core_send.at[0], core_recv.at[0], other,
        )

    def id_copy(d, src):
        return remote(idtile, idall.at[src], plane_send.at[0, d], plane_recv.at[0, src], peer(d))

    def z_copy(phase):
        if phase == 0:
            rows = pl.ds(pl.multiple_of(8 * zh, 8), 8)
            theirs = pl.ds(pl.multiple_of(8 * (1 - zh), 8), 8)
            return (
                remote(base, st.at[0, :, rows, :], zsend.at[0], zrec.at[0], across),
                remote(base, st.at[0, :, theirs, :], zsend.at[0], zrec.at[0], across),
            )
        both = remote(st.at[phase], zrecv.at[phase - 1], zsend.at[phase], zrec.at[phase], across)
        return both, both

    def g_copy(phase, d, src):
        return remote(
            gbuf.at[phase, d],
            bs.at[phase, :, pl.ds(pl.multiple_of(c * 256 + src * 16, 16), 16), :],
            plane_send.at[1 + phase, d], plane_recv.at[1 + phase, src], peer(d),
        )

    def half_copy(phase, side):
        rows = pl.ds(pl.multiple_of(side * 256, 256), 256)
        return remote(
            bs.at[phase, :, rows, :], bs.at[phase, :, rows, :],
            core_send.at[1 + phase], core_recv.at[1 + phase], other,
        )

    def p_copy(phase):
        rows = pl.ds(pl.multiple_of((1 - c) * 256, 256), 256)
        return remote(
            pbuf.at[phase, :, rows, :], prec.at[phase], core_send.at[4 + phase], core_recv.at[4 + phase], other
        )

    def r_copy(phase, d, src):
        return remote(
            rsend.at[phase, :, pl.ds(pl.multiple_of(d * 16, 16), 16), :],
            rrecv.at[phase, src],
            plane_send.at[4 + phase, d], plane_recv.at[4 + phase, src], peer(d),
        )

    def end_copy(phase, ch):
        return remote(own.at[phase, ch], erecv.at[phase, ch], line_send.at[phase, 0, ch], line_recv.at[phase, 0, ch], pair)

    def mid_copy(phase, ch):
        return remote(
            own.at[phase, ch], mrecv.at[phase, ch], line_send.at[phase, 1, ch], line_recv.at[phase, 1, ch], middle
        )

    def total_copy(phase, ch):
        return remote(tot.at[phase, ch], tot.at[phase, ch], line_send.at[phase, 2, ch], line_recv.at[phase, 2, ch], pair)

    def factor_copy(which, slot):
        return remote(
            linv.at[which, slot], linv.at[which, slot], core_send.at[6 + which], core_recv.at[6 + which], other
        )

    def y_copy(side):
        rows = pl.ds(pl.multiple_of(side * 4, 4), 4)
        return remote(y3.at[rows], y3.at[rows], core_send.at[8], core_recv.at[8], other)

    x_copy(c).start()
    z_copy(0)[0].start()
    each_peer(lambda d: id_copy(d, q).start())
    st[0, :, pl.ds(pl.multiple_of(8 * zh, 8), 8), :] = base[...]
    xw[pl.ds(pl.multiple_of(c * 256, 256), 256), :] = frames[:, pl.ds(pl.multiple_of(c * 512, 128), 512)]

    def slot_of(row):
        return jnp.where(ids[row] == first_id, 0, 1)

    def share(phase):
        def fill(d, _):
            for s in range(2):
                which = idall[d, s : s + 1, :]
                value = jnp.zeros((16, K), F32)
                for a in range(ANN):
                    value = jnp.where(which == a, st[phase, a], value)
                gbuf[phase, d, s] = value
            return 0

        lax.fori_loop(0, NPL, fill, 0)
        each_peer(lambda d: g_copy(phase, d, q).start())
        bs[phase, :, pl.ds(pl.multiple_of(c * 256 + q * 16, 16), 16), :] = gbuf[phase, q]
        each_peer(lambda d: g_copy(phase, d, d).wait_recv())
        half_copy(phase, c).start()
        half_copy(phase, 1 - c).wait_recv()

    def line_sum(phase, count):
        @pl.when(is_mid)
        def _():
            def meet(ch, _):
                end_copy(phase, ch).wait_recv()
                own[phase, ch] = own[phase, ch] + erecv[phase, ch]
                mid_copy(phase, ch).start()
                return 0

            def finish(ch, _):
                mid_copy(phase, ch).wait_recv()
                tot[phase, ch] = own[phase, ch] + mrecv[phase, ch]
                total_copy(phase, ch).start()
                return 0

            def step(ch, _):
                meet(ch, 0)
                finish(ch - 1, 0)
                return 0

            meet(0, 0)
            lax.fori_loop(1, count, step, 0)
            finish(count - 1, 0)

        @pl.when(is_end)
        def _():
            def take(ch, _):
                total_copy(phase, ch).wait_recv()
                return 0

            lax.fori_loop(0, count, take, 0)

    def chunk_done(phase, ch):
        @pl.when(is_end)
        def _():
            end_copy(phase, ch).start()

    def project(phase, source):
        for s in range(2):
            high, low = split(source[s])
            bh[s] = high
            bl[s] = low
        skip = 0
        if phase > 0:
            skip = 2
            mine = source[c]
            flipped = mine.T
            for half in range(2):
                own[phase, half] = dot_full(flipped[128 * half : 128 * half + 128, :], mine)
                chunk_done(phase, half)

        def chunk(r, _):
            rows = pl.ds(pl.multiple_of(r * 128, 128), 128)
            s = slot_of(4 * c + r)
            own[phase, skip + r] = dot3(xth[rows, :], xtl[rows, :], bh[s], bl[s])
            chunk_done(phase, skip + r)
            return 0

        lax.fori_loop(0, 4, chunk, 0)
        line_sum(phase, skip + 4)

    def back(phase, between):
        skip = 2 if phase > 0 else 0

        def mask(r, _):
            rows = pl.ds(pl.multiple_of(r * 128, 128), 128)
            s = slot_of(4 * c + r)
            high, low = split(tot[phase, skip + r])
            none = jnp.zeros((128, K), BF16)
            ymh[0, rows, :] = jnp.where(s == 0, high, none)
            yml[0, rows, :] = jnp.where(s == 0, low, none)
            ymh[1, rows, :] = jnp.where(s == 1, high, none)
            yml[1, rows, :] = jnp.where(s == 1, low, none)
            return 0

        lax.fori_loop(0, 4, mask, 0)

        def multiply(i, _):
            for s in range(2):
                rows = pl.ds(pl.multiple_of(i * 128, 128), 128)
                pbuf[phase, s, rows, :] = dot3(xh[rows, :], xl[rows, :], ymh[s], yml[s])
            return 0

        lax.fori_loop(0, 4, multiply, 0)
        p_copy(phase).start()
        p_copy(phase).wait_recv()
        rsend[phase] = pbuf[phase, :, pl.ds(pl.multiple_of(c * 256, 256), 256), :] + prec[phase]
        each_peer(lambda d: r_copy(phase, d, q).start())
        rrecv[phase, q] = rsend[phase, :, pl.ds(pl.multiple_of(q * 16, 16), 16), :]
        between()
        each_peer(lambda d: r_copy(phase, d, d).wait_recv())

        def add(src, sums):
            new = list(sums)
            for s in range(2):
                which = idall[src, s : s + 1, :]
                value = rrecv[phase, src, s]
                for a in range(ANN):
                    new[a] = new[a] + jnp.where(which == a, value, 0.0)
            return tuple(new)

        sums = lax.fori_loop(0, NPL, add, tuple(jnp.zeros((16, K), F32) for _ in range(ANN)))
        for a in range(ANN):
            st[phase + 1, a] = sums[a]
        z_copy(phase + 1)[0].start()
        z_copy(phase + 1)[1].wait()
        for a in range(ANN):
            st[phase + 1, a] = sums[a] + zrecv[phase, a]

    x_copy(1 - c).wait_recv()

    def layouts(i, _):
        rows = pl.ds(pl.multiple_of(i * 128, 128), 128)
        block = xw[rows, :]
        high, low = split(block)
        xh[rows, :] = high
        xl[rows, :] = low
        turned = block.T
        high, low = split(turned)
        xth[:, rows] = high
        xtl[:, rows] = low
        return 0

    lax.fori_loop(0, 4, layouts, 0)
    z_copy(0)[1].wait_recv()
    each_peer(lambda d: id_copy(d, d).wait_recv())

    share(0)
    project(0, bs.at[0])
    back(0, lambda: None)
    share(1)

    project(1, bs.at[1])

    def factor(which):
        smat[0:128, :] = tot[1 + which, 0]
        smat[128:256, :] = tot[1 + which, 1]
        inverse_factor(smat, linv.at[which, c])
        factor_copy(which, c).start()

    back(1, lambda: factor(0))
    share(2)
    factor_copy(0, 1 - c).wait_recv()

    def normalise(i, _):
        rows = pl.ds(pl.multiple_of(i * 256, 256), 256)
        for s in range(2):
            zb[s, rows, :] = dot_full(bs[2, s, rows, :], linv[0, s], NT)
        return 0

    lax.fori_loop(0, 2, normalise, 0)

    project(2, zb)
    y3[pl.ds(pl.multiple_of(c * 4, 4), 4)] = tot[2, 2:6]
    y_copy(c).start()
    factor(1)
    y_copy(1 - c).wait_recv()
    factor_copy(1, 1 - c).wait_recv()
    for s in range(2):
        basis = dot_full(zb[s, pl.ds(pl.multiple_of(c * 256, 256), 256), :], linv[1, s], NT)
        high, low = split(basis)
        bh[s, 0:256, :] = high
        bl[s, 0:256, :] = low
        high, low = split(linv[1, s])
        bh[s, 256:512, :] = high
        bl[s, 256:512, :] = low

    def clean(r, _):
        s = slot_of(r)
        high, low = split(y3[r])
        coefficients = dot3(high, low, bh[s, 256:512, :], bl[s, 256:512, :], NT)
        high, low = split(coefficients)
        columns = pl.ds(pl.multiple_of(r * 128, 128), 128)
        out[:, columns] = frames[:, columns] - dot3(bh[s, 0:256, :], bl[s, 0:256, :], high, low, NT)
        return 0

    lax.fori_loop(0, 8, clean, 0)

    x_copy(c).wait_send()
    z_copy(0)[0].wait_send()
    y_copy(c).wait_send()
    each_peer(lambda d: id_copy(d, q).wait_send())
    for phase in range(3):
        each_peer(lambda d: g_copy(phase, d, q).wait_send())
        half_copy(phase, c).wait_send()
    for phase in range(2):
        each_peer(lambda d: r_copy(phase, d, q).wait_send())
        p_copy(phase).wait_send()
        factor_copy(phase, c).wait_send()
    for phase in range(3):
        count = 6 if phase > 0 else 4

        @pl.when(is_mid)
        def _():
            def sent(ch, _):
                mid_copy(phase, ch).wait_send()
                total_copy(phase, ch).wait_send()
                return 0

            lax.fori_loop(0, count, sent, 0)

        @pl.when(is_end)
        def _():
            def sent(ch, _):
                end_copy(phase, ch).wait_send()
                return 0

            lax.fori_loop(0, count, sent, 0)


def solution(mesh):
    def step(frames, ann_rows, start_bases):
        vmem = pl.BlockSpec(memory_space=pltpu.VMEM)
        dma = pltpu.SemaphoreType.DMA
        return pl.pallas_call(
            kernel,
            out_shape=jax.ShapeDtypeStruct(frames.shape, F32),
            in_specs=[vmem, pl.BlockSpec(memory_space=pltpu.SMEM), vmem],
            out_specs=vmem,
            scratch_shapes=[
                pltpu.VMEM((512, 512), F32),
                pltpu.VMEM((512, 512), BF16),
                pltpu.VMEM((512, 512), BF16),
                pltpu.VMEM((512, 512), BF16),
                pltpu.VMEM((512, 512), BF16),
                pltpu.VMEM((3, 2, 512, K), F32),
                pltpu.VMEM((2, 512, K), BF16),
                pltpu.VMEM((2, 512, K), BF16),
                pltpu.VMEM((2, 512, K), F32),
                pltpu.VMEM((3, 6, 128, K), F32),
                pltpu.VMEM((3, 6, 128, K), F32),
                pltpu.VMEM((3, 6, 128, K), F32),
                pltpu.VMEM((3, 6, 128, K), F32),
                pltpu.VMEM((2, 512, K), BF16),
                pltpu.VMEM((2, 512, K), BF16),
                pltpu.VMEM((2, 2, 512, K), F32),
                pltpu.VMEM((2, 2, 256, K), F32),
                pltpu.VMEM((2, 2, 256, K), F32),
                pltpu.VMEM((2, NPL, 2, 16, K), F32),
                pltpu.VMEM((3, ANN, 16, K), F32),
                pltpu.VMEM((2, ANN, 16, K), F32),
                pltpu.VMEM((3, NPL, 2, 16, K), F32),
                pltpu.VMEM((8, K), jnp.int32),
                pltpu.VMEM((NPL, 8, K), jnp.int32),
                pltpu.VMEM((K, K), F32),
                pltpu.VMEM((2, 2, K, K), F32),
                pltpu.VMEM((8, 128, K), F32),
                pltpu.VMEM((8, 128), F32),
                dma((9,)), dma((9,)),
                dma((6, NPL)), dma((6, NPL)),
                dma((3,)), dma((3,)),
                dma((3, 3, 6)), dma((3, 3, 6)),
            ],
            compiler_params=pltpu.CompilerParams(
                collective_id=0, has_side_effects=True, vmem_limit_bytes=56 * 1024 * 1024
            ),
        )(frames, ann_rows, start_bases)

    return jax.shard_map(
        step,
        mesh=mesh,
        in_specs=(P("tm", "pix"), P("pix"), P(None, ("tm", "pix"), None)),
        out_specs=P("tm", "pix"),
        check_vma=False,
    )
```

```python
import jax
import jax.numpy as jnp
from jax import lax
from jax.experimental import pallas as pl
from jax.experimental.pallas import tpu as pltpu
from jax.sharding import PartitionSpec as P

MESH = pl.DeviceIdType.MESH
F32 = jnp.float32
BF16 = jnp.bfloat16
HIGHEST = lax.Precision.HIGHEST
ANN = 4
K = 256
H = K // 2
NPL = 16
CHUNKS = 11
NN = (((1,), (0,)), ((), ()))
NT = (((1,), (1,)), ((), ()))


def dot(a, b, dims=NN):
    return lax.dot_general(a, b, dims, preferred_element_type=F32)


def dot_full(a, b, dims=NN):
    return lax.dot_general(a, b, dims, precision=HIGHEST, preferred_element_type=F32)


def split(a):
    high = a.astype(BF16)
    return high, (a - high.astype(F32)).astype(BF16)


def dot3(ah, al, bh, bl, dims=NN):
    return dot(ah, bh, dims) + (dot(ah, bl, dims) + dot(al, bh, dims))


def leaf(a, result):
    n = 128
    groups = n // 8
    sub = lax.broadcasted_iota(jnp.int32, (8, n), 0)
    lane = lax.broadcasted_iota(jnp.int32, (8, n), 1)
    left = [a[8 * g : 8 * g + 8, :] for g in range(groups)]
    right = [jnp.where(lane == sub + 8 * g, 1.0, 0.0).astype(F32) for g in range(groups)]
    done = []
    for g0 in range(groups):
        k0 = 8 * g0
        rows_left, rows_right, scaled = [], [], []
        own_left, own_right = left[g0], right[g0]
        columns = [jnp.broadcast_to(own_left[:, k0 + j : k0 + j + 1], (8, n)) for j in range(8)]
        final = jnp.zeros((8, n), F32)
        for j in range(8):
            pivot = columns[j][j : j + 1, :]
            inverse = 1.0 / pivot
            final = jnp.where(sub == j, own_right * lax.rsqrt(pivot), final)
            rows_left.append(own_left[j : j + 1, :] * inverse)
            rows_right.append(own_right[j : j + 1, :] * inverse)
            scaled.append([columns[i][j : j + 1, :] * inverse for i in range(j + 1, 8)])
            if j < 7:
                below = jnp.where(sub > j, columns[j], 0.0)
                own_left = own_left - below * rows_left[j]
                own_right = own_right - below * rows_right[j]
                for i in range(j + 1, 8):
                    columns[i] = columns[i] - below * scaled[j][i - j - 1]
        done.append(final)
        for g in range(g0 + 1, groups):
            columns = [jnp.broadcast_to(left[g][:, k0 + j : k0 + j + 1], (8, n)) for j in range(8)]
            new_left, new_right = left[g], right[g]
            for j in range(8):
                new_left = new_left - columns[j] * rows_left[j]
                new_right = new_right - columns[j] * rows_right[j]
                for i in range(j + 1, 8):
                    columns[i] = columns[i] - columns[j] * scaled[j][i - j - 1]
            left[g], right[g] = new_left, new_right
        yield
    result.append(jnp.concatenate(done, 0))


def inverse_factor(s00, s10, s11, out_ref):
    leaves = []
    yield from leaf(s00[...], leaves)
    first = leaves[0]
    out_ref[0:128, 0:128] = first
    out_ref[0:128, 128:256] = jnp.zeros((128, 128), F32)
    lower = dot_full(s10[...], first, NT)
    yield from leaf(s11[...] - dot_full(lower, lower, NT), leaves)
    second = leaves[1]
    out_ref[128:256, 128:256] = second
    out_ref[128:256, 0:128] = -dot_full(second, dot_full(lower, out_ref[0:128, 0:128]))


def advance(steps, count):
    for _ in range(count):
        next(steps, None)


def kernel(
    frames, ids, base, out,
    xw, xh, xl, xth, xtl, bs, bh, bl, zb,
    own, erecv, mrecv, tot, ymh, yml,
    pbuf, prec, rsend, rrecv, st, zrecv, gbuf, idtile, idall,
    linv, y3, base0,
    core_send, core_recv, plane_send, plane_recv, zsend, zrec, line_send, line_recv,
):
    t, p = lax.axis_index("tm"), lax.axis_index("pix")
    c, zl = lax.rem(t, 2), t // 2
    q, zh = p // 2, lax.rem(p, 2)
    is_mid = jnp.logical_or(zl == 1, zl == 2)
    is_end = jnp.logical_or(zl == 0, zl == 3)
    other = {"tm": t + 1 - 2 * c, "pix": p}
    across = {"tm": t, "pix": 2 * q + 1 - zh}
    pair = {"tm": 2 * (zl + 1 - 2 * lax.rem(zl, 2)) + c, "pix": p}
    middle = {"tm": 2 * (3 - zl) + c, "pix": p}

    def peer(d):
        return {"tm": t, "pix": 2 * d + zh}

    def remote(src, dst, send, recv, device):
        return pltpu.make_async_remote_copy(
            src_ref=src, dst_ref=dst, send_sem=send, recv_sem=recv, device_id=device, device_id_type=MESH
        )

    def greet(device):
        pl.semaphore_signal(barrier, inc=1, device_id=device, device_id_type=MESH)

    def each_peer(body):
        def step(d, _):
            body(lax.rem(q + d, NPL))
            return 0

        lax.fori_loop(1, NPL, step, 0)

    def part(index, size):
        return pl.ds(pl.multiple_of(index * size, size), size)

    barrier = pltpu.get_barrier_semaphore()
    greet(other)
    greet(across)
    greet(pair)
    each_peer(lambda d: greet(peer(d)))

    @pl.when(is_mid)
    def _():
        greet(middle)

    first_id, last_id = ids[0], ids[7]
    idtile[:, 0:H] = jnp.full((8, H), first_id, jnp.int32)
    idtile[:, H:K] = jnp.full((8, H), last_id, jnp.int32)
    idall[q] = idtile[...]
    for half in range(2):
        base0[half] = base[:, :, half * H : half * H + H]
    pl.semaphore_wait(barrier, jnp.where(is_mid, 19, 18))

    def x_copy(side):
        return remote(frames.at[:, part(1 - c, 512)], xw.at[part(side, 256), :], core_send.at[0], core_recv.at[0], other)

    def id_copy(d, src):
        return remote(idtile, idall.at[src], plane_send.at[0, d], plane_recv.at[0, src], peer(d))

    def base_copy(side):
        return remote(base0, st.at[0, :, :, part(side, 8), :], zsend.at[0], zrec.at[0], across)

    def z_copy(phase, half):
        k = 2 * phase + half - 1
        return remote(st.at[phase, half], zrecv.at[phase - 1, half], zsend.at[k], zrec.at[k], across)

    def g_copy(phase, half, d, src):
        k = 1 + 2 * phase + half
        return remote(
            gbuf.at[phase, half, d],
            bs.at[phase, half, pl.ds(pl.multiple_of(c * 256 + src * 16, 16), 16), :],
            plane_send.at[k, d], plane_recv.at[k, src], peer(d),
        )

    def half_copy(phase, half, side):
        k = 1 + 2 * phase + half
        rows = bs.at[phase, half, part(side, 256), :]
        return remote(rows, rows, core_send.at[k], core_recv.at[k], other)

    def p_copy(phase, half):
        k = 7 + 2 * phase + half
        return remote(
            pbuf.at[phase, half, part(1 - c, 256), :], prec.at[phase, half], core_send.at[k], core_recv.at[k], other
        )

    def r_copy(phase, half, d, src):
        k = 7 + 2 * phase + half
        return remote(
            rsend.at[phase, half, part(d, 16), :], rrecv.at[phase, half, src],
            plane_send.at[k, d], plane_recv.at[k, src], peer(d),
        )

    def end_copy(phase, ch):
        return remote(own.at[phase, ch], erecv.at[phase, ch], line_send.at[phase, 0, ch], line_recv.at[phase, 0, ch], pair)

    def mid_copy(phase, ch):
        return remote(
            own.at[phase, ch], mrecv.at[phase, ch], line_send.at[phase, 1, ch], line_recv.at[phase, 1, ch], middle
        )

    def total_copy(phase, ch):
        return remote(tot.at[phase, ch], tot.at[phase, ch], line_send.at[phase, 2, ch], line_recv.at[phase, 2, ch], pair)

    def factor_copy(which, slot):
        return remote(
            linv.at[which, slot], linv.at[which, slot], core_send.at[11 + which], core_recv.at[11 + which], other
        )

    def y_copy(half, side):
        rows = y3.at[half, part(side, 4)]
        return remote(rows, rows, core_send.at[13 + half], core_recv.at[13 + half], other)

    base_copy(zh).start()
    each_peer(lambda d: id_copy(d, q).start())
    x_copy(c).start()
    st[0, :, :, part(zh, 8), :] = base0[...]
    xw[part(c, 256), :] = frames[:, part(c, 512)]

    def slot_of(row):
        return jnp.where(ids[row] == first_id, 0, 1)

    def share(phase, half):
        def fill(d, _):
            which = idall[d, 0:1, :]
            value = jnp.zeros((16, K), F32)
            for a in range(ANN):
                rows = st[phase, half, a]
                value = jnp.where(which == a, jnp.concatenate([rows, rows], 1), value)
            gbuf[phase, half, d] = value
            return 0

        lax.fori_loop(0, NPL, fill, 0)
        each_peer(lambda d: g_copy(phase, half, d, q).start())
        bs[phase, half, pl.ds(pl.multiple_of(c * 256 + q * 16, 16), 16), :] = gbuf[phase, half, q]

    def shared(phase, half):
        each_peer(lambda d: g_copy(phase, half, d, d).wait_recv())
        half_copy(phase, half, c).start()

    def send_own(phase, ch):
        @pl.when(is_end)
        def _():
            end_copy(phase, ch).start()

    def relay(phase, meet, finish, take):
        @pl.when(is_mid)
        def _():
            for ch in meet:
                end_copy(phase, ch).wait_recv()
                own[phase, ch] = own[phase, ch] + erecv[phase, ch]
                mid_copy(phase, ch).start()
            for ch in finish:
                mid_copy(phase, ch).wait_recv()
                tot[phase, ch] = own[phase, ch] + mrecv[phase, ch]
                total_copy(phase, ch).start()

        @pl.when(is_end)
        def _():
            for ch in take:
                total_copy(phase, ch).wait_recv()

    def project(phase, half, source):
        high, low = split(source[...])
        bh[half] = high
        bl[half] = low

        def chunk(r, _):
            rows = part(r, 128)
            both = dot3(xth[rows, :], xtl[rows, :], bh[half], bl[half])
            own[phase, 4 * half + r] = jnp.where(slot_of(4 * c + r) == 0, both[:, 0:H], both[:, H:K])
            send_own(phase, 4 * half + r)
            return 0

        lax.fori_loop(0, 4, chunk, 0)

    def squares(phase, first, second):
        first, second = first[:, part(c, H)], second[:, part(c, H)]
        turned = second.T
        own[phase, 8] = dot_full(first.T, first)
        send_own(phase, 8)
        own[phase, 9] = dot_full(turned, first)
        send_own(phase, 9)
        own[phase, 10] = dot_full(turned, second)
        send_own(phase, 10)

    def back(phase, half):
        def mask(r, _):
            rows = part(r, 128)
            slot = slot_of(4 * c + r)
            value = tot[phase, 4 * half + r]
            high, low = split(jnp.concatenate([jnp.where(slot == 0, value, 0.0), jnp.where(slot == 1, value, 0.0)], 1))
            ymh[half, rows, :] = high
            yml[half, rows, :] = low
            return 0

        lax.fori_loop(0, 4, mask, 0)

        def multiply(i, _):
            rows = part(i, 256)
            pbuf[phase, half, rows, :] = dot3(xh[rows, :], xl[rows, :], ymh[half], yml[half])
            return 0

        lax.fori_loop(0, 2, multiply, 0)
        p_copy(phase, half).start()

    def scatter(phase, half):
        p_copy(phase, half).wait_recv()
        rsend[phase, half] = pbuf[phase, half, part(c, 256), :] + prec[phase, half]
        each_peer(lambda d: r_copy(phase, half, d, q).start())
        rrecv[phase, half, q] = rsend[phase, half, part(q, 16), :]

    def combine(phase, half):
        each_peer(lambda d: r_copy(phase, half, d, d).wait_recv())

        def add(src, sums):
            which = idall[src, 0:1, :]
            value = rrecv[phase, half, src]
            new = []
            for a in range(ANN):
                kept = jnp.where(which == a, value, 0.0)
                new.append(sums[a] + (kept[:, 0:H] + kept[:, H:K]))
            return tuple(new)

        sums = lax.fori_loop(0, NPL, add, tuple(jnp.zeros((16, H), F32) for _ in range(ANN)))
        for a in range(ANN):
            st[phase + 1, half, a] = sums[a]
        z_copy(phase + 1, half).start()

    def settle(phase, half):
        z_copy(phase, half).wait()
        st[phase, half] = st[phase, half] + zrecv[phase - 1, half]

    x_copy(1 - c).wait_recv()

    def layouts(i, _):
        rows = part(i, 128)
        block = xw[rows, :]
        high, low = split(block)
        xh[rows, :] = high
        xl[rows, :] = low
        high, low = split(block.T)
        xth[:, rows] = high
        xtl[:, rows] = low
        return 0

    lax.fori_loop(0, 4, layouts, 0)
    base_copy(1 - zh).wait_recv()
    each_peer(lambda d: id_copy(d, d).wait_recv())
    for half in range(2):
        share(0, half)

    factor = iter(())
    for phase in range(2):
        for half in range(2):
            shared(phase, half)
        for half in range(2):
            half_copy(phase, half, 1 - c).wait_recv()
            project(phase, half, bs.at[phase, half])
        relay(phase, [0, 1], [], [])
        if phase == 1:
            squares(1, bs.at[1, 0], bs.at[1, 1])
        relay(phase, [2], [0], [])
        relay(phase, [3], [1], [])
        relay(phase, [4], [2], [])
        relay(phase, [5], [3], [0, 1, 2, 3])
        back(phase, 0)
        relay(phase, [6], [4], [])
        relay(phase, [7], [5], [])
        if phase == 1:
            relay(phase, [8], [6], [])
            relay(phase, [9], [7], [4, 5, 6, 7])
        else:
            relay(phase, [], [6, 7], [4, 5, 6, 7])
        back(phase, 1)
        if phase == 1:
            relay(phase, [10], [8], [])
        scatter(phase, 0)
        if phase == 1:
            relay(phase, [], [9, 10], [])
        scatter(phase, 1)
        if phase == 1:
            relay(phase, [], [], [8, 9, 10])
            factor = inverse_factor(tot.at[1, 8], tot.at[1, 9], tot.at[1, 10], linv.at[0, c])
        advance(factor, 10)
        for half in range(2):
            combine(phase, half)
        advance(factor, 10)
        for half in range(2):
            settle(phase + 1, half)
            share(phase + 1, half)
        advance(factor, 100)
    factor_copy(0, c).start()

    for half in range(2):
        shared(2, half)
    factor_copy(0, 1 - c).wait_recv()
    for half in range(2):
        half_copy(2, half, 1 - c).wait_recv()

    def normalise(i, _):
        rows = part(i, 256)
        for s in range(2):
            lanes = slice(s * H, s * H + H)
            product = jnp.concatenate([bs[2, 0, rows, lanes], bs[2, 1, rows, lanes]], 1)
            new = dot_full(product, linv[0, s], NT)
            zb[0, rows, lanes] = new[:, 0:H]
            zb[1, rows, lanes] = new[:, H:K]
        return 0

    lax.fori_loop(0, 2, normalise, 0)

    squares(2, zb.at[0], zb.at[1])
    for half in range(2):
        project(2, half, zb.at[half])
    relay(2, [8, 9], [], [])
    relay(2, [10], [8], [])
    relay(2, [0], [9], [])
    relay(2, [1], [10], [8, 9, 10])
    factor = inverse_factor(tot.at[2, 8], tot.at[2, 9], tot.at[2, 10], linv.at[1, c])
    advance(factor, 2)
    for step in range(2, 8):
        relay(2, [step], [step - 2], [step - 2])
        advance(factor, 3)
    relay(2, [], [6], [6])
    advance(factor, 2)
    relay(2, [], [7], [7])
    for half in range(2):
        y3[half, part(c, 4)] = tot[2, 4 * half : 4 * half + 4]
        y_copy(half, c).start()
    advance(factor, 100)
    factor_copy(1, c).start()
    for half in range(2):
        y_copy(half, 1 - c).wait_recv()
    factor_copy(1, 1 - c).wait_recv()
    for s in range(2):
        lanes = slice(s * H, s * H + H)
        vectors = jnp.concatenate([zb[0, part(c, 256), lanes], zb[1, part(c, 256), lanes]], 1)
        high, low = split(dot_full(vectors, linv[1, s], NT))
        bh[s, 0:256, :] = high
        bl[s, 0:256, :] = low
        high, low = split(linv[1, s])
        bh[s, 256:512, :] = high
        bl[s, 256:512, :] = low

    def clean(r, _):
        s = slot_of(r)
        high, low = split(jnp.concatenate([y3[0, r], y3[1, r]], 1))
        coefficients = dot3(high, low, bh[s, 256:512, :], bl[s, 256:512, :], NT)
        high, low = split(coefficients)
        columns = part(r, 128)
        out[:, columns] = frames[:, columns] - dot3(bh[s, 0:256, :], bl[s, 0:256, :], high, low, NT)
        return 0

    lax.fori_loop(0, 8, clean, 0)

    x_copy(c).wait_send()
    base_copy(zh).wait_send()
    each_peer(lambda d: id_copy(d, q).wait_send())
    for half in range(2):
        y_copy(half, c).wait_send()
        factor_copy(half, c).wait_send()
        for phase in range(3):
            each_peer(lambda d: g_copy(phase, half, d, q).wait_send())
            half_copy(phase, half, c).wait_send()
        for phase in range(2):
            each_peer(lambda d: r_copy(phase, half, d, q).wait_send())
            p_copy(phase, half).wait_send()
    for phase in range(3):
        count = 11 if phase > 0 else 8

        @pl.when(is_mid)
        def _():
            def sent(ch, _):
                mid_copy(phase, ch).wait_send()
                total_copy(phase, ch).wait_send()
                return 0

            lax.fori_loop(0, count, sent, 0)

        @pl.when(is_end)
        def _():
            def sent(ch, _):
                end_copy(phase, ch).wait_send()
                return 0

            lax.fori_loop(0, count, sent, 0)


def solution(mesh):
    def step(frames, ann_rows, start_bases):
        vmem = pl.BlockSpec(memory_space=pltpu.VMEM)
        dma = pltpu.SemaphoreType.DMA
        return pl.pallas_call(
            kernel,
            out_shape=jax.ShapeDtypeStruct(frames.shape, F32),
            in_specs=[vmem, pl.BlockSpec(memory_space=pltpu.SMEM), vmem],
            out_specs=vmem,
            scratch_shapes=[
                pltpu.VMEM((512, 512), F32),
                pltpu.VMEM((512, 512), BF16),
                pltpu.VMEM((512, 512), BF16),
                pltpu.VMEM((512, 512), BF16),
                pltpu.VMEM((512, 512), BF16),
                pltpu.VMEM((3, 2, 512, K), F32),
                pltpu.VMEM((2, 512, K), BF16),
                pltpu.VMEM((2, 512, K), BF16),
                pltpu.VMEM((2, 512, K), F32),
                pltpu.VMEM((3, CHUNKS, 128, H), F32),
                pltpu.VMEM((3, CHUNKS, 128, H), F32),
                pltpu.VMEM((3, CHUNKS, 128, H), F32),
                pltpu.VMEM((3, CHUNKS, 128, H), F32),
                pltpu.VMEM((2, 512, K), BF16),
                pltpu.VMEM((2, 512, K), BF16),
                pltpu.VMEM((2, 2, 512, K), F32),
                pltpu.VMEM((2, 2, 256, K), F32),
                pltpu.VMEM((2, 2, 256, K), F32),
                pltpu.VMEM((2, 2, NPL, 16, K), F32),
                pltpu.VMEM((3, 2, ANN, 16, H), F32),
                pltpu.VMEM((2, 2, ANN, 16, H), F32),
                pltpu.VMEM((3, 2, NPL, 16, K), F32),
                pltpu.VMEM((8, K), jnp.int32),
                pltpu.VMEM((NPL, 8, K), jnp.int32),
                pltpu.VMEM((2, 2, K, K), F32),
                pltpu.VMEM((2, 8, 128, H), F32),
                pltpu.VMEM((2, ANN, 8, H), F32),
                dma((15,)), dma((15,)),
                dma((11, NPL)), dma((11, NPL)),
                dma((5,)), dma((5,)),
                dma((3, 3, CHUNKS)), dma((3, 3, CHUNKS)),
            ],
            compiler_params=pltpu.CompilerParams(
                collective_id=0, has_side_effects=True, vmem_limit_bytes=56 * 1024 * 1024
            ),
        )(frames, ann_rows, start_bases)

    return jax.shard_map(
        step,
        mesh=mesh,
        in_specs=(P("tm", "pix"), P("pix"), P(None, ("tm", "pix"), None)),
        out_specs=P("tm", "pix"),
        check_vma=False,
    )
```

```python
import jax
import jax.numpy as jnp
from jax import lax
from jax.experimental import pallas as pl
from jax.experimental.pallas import tpu as pltpu
from jax.sharding import PartitionSpec as P

MESH = pl.DeviceIdType.MESH
F32 = jnp.float32
BF16 = jnp.bfloat16
HIGHEST = lax.Precision.HIGHEST
ANN = 4
K = 256
H = K // 2
NPL = 16
CHUNKS = 11
NN = (((1,), (0,)), ((), ()))
NT = (((1,), (1,)), ((), ()))


def dot(a, b, dims=NN):
    return lax.dot_general(a, b, dims, preferred_element_type=F32)


def dot_full(a, b, dims=NN):
    return lax.dot_general(a, b, dims, precision=HIGHEST, preferred_element_type=F32)


def split(a):
    high = a.astype(BF16)
    return high, (a - high.astype(F32)).astype(BF16)


def dot3(ah, al, bh, bl, dims=NN):
    return dot(ah, bh, dims) + (dot(ah, bl, dims) + dot(al, bh, dims))


def leaf(a, result):
    n = 128
    groups = n // 8
    sub = lax.broadcasted_iota(jnp.int32, (8, n), 0)
    lane = lax.broadcasted_iota(jnp.int32, (8, n), 1)
    left = [a[8 * g : 8 * g + 8, :] for g in range(groups)]
    right = [jnp.where(lane == sub + 8 * g, 1.0, 0.0).astype(F32) for g in range(groups)]
    done = []
    for g0 in range(groups):
        k0 = 8 * g0
        rows_left, rows_right, scaled = [], [], []
        own_left, own_right = left[g0], right[g0]
        columns = [jnp.broadcast_to(own_left[:, k0 + j : k0 + j + 1], (8, n)) for j in range(8)]
        final = jnp.zeros((8, n), F32)
        for j in range(8):
            pivot = columns[j][j : j + 1, :]
            inverse = 1.0 / pivot
            final = jnp.where(sub == j, own_right * lax.rsqrt(pivot), final)
            rows_left.append(own_left[j : j + 1, :] * inverse)
            rows_right.append(own_right[j : j + 1, :] * inverse)
            scaled.append([columns[i][j : j + 1, :] * inverse for i in range(j + 1, 8)])
            if j < 7:
                below = jnp.where(sub > j, columns[j], 0.0)
                own_left = own_left - below * rows_left[j]
                own_right = own_right - below * rows_right[j]
                for i in range(j + 1, 8):
                    columns[i] = columns[i] - below * scaled[j][i - j - 1]
        done.append(final)
        for g in range(g0 + 1, groups):
            columns = [jnp.broadcast_to(left[g][:, k0 + j : k0 + j + 1], (8, n)) for j in range(8)]
            new_left, new_right = left[g], right[g]
            for j in range(8):
                new_left = new_left - columns[j] * rows_left[j]
                new_right = new_right - columns[j] * rows_right[j]
                for i in range(j + 1, 8):
                    columns[i] = columns[i] - columns[j] * scaled[j][i - j - 1]
            left[g], right[g] = new_left, new_right
        yield
    result.append(jnp.concatenate(done, 0))


def inverse_factor(s00, s10, s11, out_ref):
    leaves = []
    yield from leaf(s00[...], leaves)
    first = leaves[0]
    out_ref[0:128, 0:128] = first
    out_ref[0:128, 128:256] = jnp.zeros((128, 128), F32)
    lower = dot_full(s10[...], first, NT)
    yield from leaf(s11[...] - dot_full(lower, lower, NT), leaves)
    second = leaves[1]
    out_ref[128:256, 128:256] = second
    out_ref[128:256, 0:128] = -dot_full(second, dot_full(lower, out_ref[0:128, 0:128]))


def advance(steps, count):
    for _ in range(count):
        next(steps, None)


def kernel(
    frames_in, ids, base_in, out,
    frames, base,
    xw, xh, xl, xth, xtl, bs, bh, bl, zb,
    own, erecv, mrecv, tot, ymh, yml,
    pbuf, prec, rsend, rrecv, st, zrecv, gbuf, idtile, idall,
    linv, y3, base0, found,
    local, core_send, core_recv, plane_send, plane_recv, zsend, zrec, line_send, line_recv,
):
    t, p = lax.axis_index("tm"), lax.axis_index("pix")
    c, zl = lax.rem(t, 2), t // 2
    q, zh = p // 2, lax.rem(p, 2)
    is_mid = jnp.logical_or(zl == 1, zl == 2)
    is_end = jnp.logical_or(zl == 0, zl == 3)
    other = {"tm": t + 1 - 2 * c, "pix": p}
    across = {"tm": t, "pix": 2 * q + 1 - zh}
    pair = {"tm": 2 * (zl + 1 - 2 * lax.rem(zl, 2)) + c, "pix": p}
    middle = {"tm": 2 * (3 - zl) + c, "pix": p}

    def peer(d):
        return {"tm": t, "pix": 2 * d + zh}

    def remote(src, dst, send, recv, device):
        return pltpu.make_async_remote_copy(
            src_ref=src, dst_ref=dst, send_sem=send, recv_sem=recv, device_id=device, device_id_type=MESH
        )

    def greet(device):
        pl.semaphore_signal(barrier, inc=1, device_id=device, device_id_type=MESH)

    def each_peer(body):
        def step(d, _):
            body(lax.rem(q + d, NPL))
            return 0

        lax.fori_loop(1, NPL, step, 0)

    def part(index, size):
        return pl.ds(pl.multiple_of(index * size, size), size)

    fetch = pltpu.make_async_copy(frames_in, frames, local.at[8])
    fetch.start()
    fetch_base = pltpu.make_async_copy(base_in, base, local.at[9])
    fetch_base.start()
    barrier = pltpu.get_barrier_semaphore()
    greet(other)
    greet(across)
    greet(pair)
    each_peer(lambda d: greet(peer(d)))

    @pl.when(is_mid)
    def _():
        greet(middle)

    first_id, last_id = ids[0], ids[7]
    idtile[:, 0:H] = jnp.full((8, H), first_id, jnp.int32)
    idtile[:, H:K] = jnp.full((8, H), last_id, jnp.int32)
    idall[q] = idtile[...]
    fetch_base.wait()
    for half in range(2):
        base0[half] = base[:, :, half * H : half * H + H]
    pl.semaphore_wait(barrier, jnp.where(is_mid, 19, 18))

    def x_copy():
        return remote(frames.at[:, part(1 - c, 512)], xw, core_send.at[0], core_recv.at[0], other)

    def id_copy(d, src):
        return remote(idtile, idall.at[src], plane_send.at[0, d], plane_recv.at[0, src], peer(d))

    def base_copy(side):
        return remote(base0, st.at[0, :, :, part(side, 8), :], zsend.at[0], zrec.at[0], across)

    def z_copy(phase, half):
        k = 2 * phase + half - 1
        return remote(st.at[phase, half], zrecv.at[phase - 1, half], zsend.at[k], zrec.at[k], across)

    def g_copy(phase, half, d, src):
        k = 1 + 2 * phase + half
        return remote(
            gbuf.at[phase, half, d],
            bs.at[phase, half, pl.ds(pl.multiple_of(c * 256 + src * 16, 16), 16), :],
            plane_send.at[k, d], plane_recv.at[k, src], peer(d),
        )

    def half_copy(phase, half, side):
        k = 1 + 2 * phase + half
        rows = bs.at[phase, half, part(side, 256), :]
        return remote(rows, rows, core_send.at[k], core_recv.at[k], other)

    def p_copy(phase, half):
        k = 7 + 2 * phase + half
        return remote(
            pbuf.at[phase, half, part(1 - c, 256), :], prec.at[phase, half], core_send.at[k], core_recv.at[k], other
        )

    def r_copy(phase, half, d, src):
        k = 7 + 2 * phase + half
        return remote(
            rsend.at[phase, half, part(d, 16), :], rrecv.at[phase, half, src],
            plane_send.at[k, d], plane_recv.at[k, src], peer(d),
        )

    def end_copy(phase, ch):
        return remote(own.at[phase, ch], erecv.at[phase, ch], line_send.at[phase, 0, ch], line_recv.at[phase, 0, ch], pair)

    def mid_copy(phase, ch):
        return remote(
            own.at[phase, ch], mrecv.at[phase, ch], line_send.at[phase, 1, ch], line_recv.at[phase, 1, ch], middle
        )

    def total_copy(phase, ch):
        return remote(tot.at[phase, ch], tot.at[phase, ch], line_send.at[phase, 2, ch], line_recv.at[phase, 2, ch], pair)

    def factor_copy(which, slot):
        return remote(
            linv.at[which, slot], linv.at[which, slot], core_send.at[11 + which], core_recv.at[11 + which], other
        )

    def y_copy(row, side):
        rows = y3.at[4 * side + row]
        return remote(rows, rows, core_send.at[13 + row], core_recv.at[13 + row], other)

    base_copy(zh).start()
    fetch.wait()
    x_copy().start()
    each_peer(lambda d: id_copy(d, q).start())
    st[0, :, :, part(zh, 8), :] = base0[...]

    def slot_of(row):
        return jnp.where(ids[row] == first_id, 0, 1)

    def share(phase, half):
        def fill(d, _):
            which = idall[d, 0:1, :]
            value = jnp.zeros((16, K), F32)
            for a in range(ANN):
                rows = st[phase, half, a]
                value = jnp.where(which == a, jnp.concatenate([rows, rows], 1), value)
            gbuf[phase, half, d] = value
            return 0

        lax.fori_loop(0, NPL, fill, 0)
        each_peer(lambda d: g_copy(phase, half, d, q).start())
        bs[phase, half, pl.ds(pl.multiple_of(c * 256 + q * 16, 16), 16), :] = gbuf[phase, half, q]

    def shared(phase, half):
        each_peer(lambda d: g_copy(phase, half, d, d).wait_recv())
        half_copy(phase, half, c).start()

    def send_own(phase, ch):
        @pl.when(is_end)
        def _():
            end_copy(phase, ch).start()

    def relay(phase, meet, finish, take):
        @pl.when(is_mid)
        def _():
            for ch in meet:
                end_copy(phase, ch).wait_recv()
                own[phase, ch] = own[phase, ch] + erecv[phase, ch]
                mid_copy(phase, ch).start()
            for ch in finish:
                mid_copy(phase, ch).wait_recv()
                tot[phase, ch] = own[phase, ch] + mrecv[phase, ch]
                total_copy(phase, ch).start()

        @pl.when(is_end)
        def _():
            for ch in take:
                total_copy(phase, ch).wait_recv()

    def project(phase, half, source):
        high, low = split(source[...])
        bh[half] = high
        bl[half] = low

        def chunk(r, _):
            rows = part(r, 128)
            both = dot3(xth[rows, :], xtl[rows, :], bh[half], bl[half])
            own[phase, 4 * half + r] = jnp.where(slot_of(4 * c + r) == 0, both[:, 0:H], both[:, H:K])
            send_own(phase, 4 * half + r)
            return 0

        lax.fori_loop(0, 4, chunk, 0)

    def squares(phase, first, second):
        first, second = first[:, part(c, H)], second[:, part(c, H)]
        turned = second.T
        own[phase, 8] = dot_full(first.T, first)
        send_own(phase, 8)
        own[phase, 9] = dot_full(turned, first)
        send_own(phase, 9)
        own[phase, 10] = dot_full(turned, second)
        send_own(phase, 10)

    def back(phase, half, step):
        for r in (2 * step, 2 * step + 1):
            rows = slice(128 * r, 128 * r + 128)
            slot = slot_of(4 * c + r)
            value = tot[phase, 4 * half + r]
            high, low = split(jnp.concatenate([jnp.where(slot == 0, value, 0.0), jnp.where(slot == 1, value, 0.0)], 1))
            ymh[half, rows, :] = high
            yml[half, rows, :] = low
        depth = slice(256 * step, 256 * step + 256)

        def multiply(i, _):
            rows = part(i, 256)
            product = dot3(xh[rows, depth], xl[rows, depth], ymh[half, depth, :], yml[half, depth, :])
            if step == 0:
                pbuf[phase, half, rows, :] = product
            else:
                pbuf[phase, half, rows, :] = pbuf[phase, half, rows, :] + product
            return 0

        lax.fori_loop(0, 2, multiply, 0)
        if step == 1:
            p_copy(phase, half).start()

    def scatter(phase, half):
        p_copy(phase, half).wait_recv()
        rsend[phase, half] = pbuf[phase, half, part(c, 256), :] + prec[phase, half]
        each_peer(lambda d: r_copy(phase, half, d, q).start())
        rrecv[phase, half, q] = rsend[phase, half, part(q, 16), :]

    def combine(phase, half):
        each_peer(lambda d: r_copy(phase, half, d, d).wait_recv())

        def add(src, sums):
            which = idall[src, 0:1, :]
            value = rrecv[phase, half, src]
            new = []
            for a in range(ANN):
                kept = jnp.where(which == a, value, 0.0)
                new.append(sums[a] + (kept[:, 0:H] + kept[:, H:K]))
            return tuple(new)

        sums = lax.fori_loop(0, NPL, add, tuple(jnp.zeros((16, H), F32) for _ in range(ANN)))
        for a in range(ANN):
            st[phase + 1, half, a] = sums[a]
        z_copy(phase + 1, half).start()

    def settle(phase, half):
        z_copy(phase, half).wait()
        st[phase, half] = st[phase, half] + zrecv[phase - 1, half]

    def layout(block, rows):
        high, low = split(block)
        xh[rows, :] = high
        xl[rows, :] = low
        high, low = split(block.T)
        xth[:, rows] = high
        xtl[:, rows] = low

    def layout_own(i, _):
        layout(frames[part(i, 128), part(c, 512)], part(2 * c + i, 128))
        return 0

    def layout_other(i, _):
        layout(xw[part(i, 128), :], part(2 * (1 - c) + i, 128))
        return 0

    lax.fori_loop(0, 2, layout_own, 0)
    x_copy().wait_recv()
    lax.fori_loop(0, 2, layout_other, 0)
    base_copy(1 - zh).wait_recv()
    each_peer(lambda d: id_copy(d, d).wait_recv())
    for half in range(2):
        share(0, half)

    def received(phase, half):
        half_copy(phase, half, 1 - c).wait_recv()

    factor = iter(())
    for phase in range(2):
        last = phase == 1
        shared(phase, 0)
        received(phase, 0)
        project(phase, 0, bs.at[phase, 0])
        shared(phase, 1)
        relay(phase, [0, 1], [], [])
        received(phase, 1)
        project(phase, 1, bs.at[phase, 1])
        relay(phase, [2], [], [])
        relay(phase, [3], [0], [])
        if last:
            squares(1, bs.at[1, 0], bs.at[1, 1])
        relay(phase, [4], [1], [0, 1])
        back(phase, 0, 0)
        relay(phase, [5], [2], [])
        relay(phase, [6], [3], [2, 3])
        back(phase, 0, 1)
        relay(phase, [7], [4], [])
        relay(phase, [8] if last else [], [5], [])
        scatter(phase, 0)
        relay(phase, [9] if last else [], [6], [4, 5])
        back(phase, 1, 0)
        relay(phase, [10] if last else [], [7], [6, 7])
        back(phase, 1, 1)
        if last:
            relay(1, [], [8], [])
        combine(phase, 0)
        if last:
            relay(1, [], [9, 10], [])
        scatter(phase, 1)
        if last:
            relay(1, [], [], [8, 9, 10])
            factor = inverse_factor(tot.at[1, 8], tot.at[1, 9], tot.at[1, 10], linv.at[0, c])
        advance(factor, 6)
        settle(phase + 1, 0)
        share(phase + 1, 0)
        advance(factor, 6)
        combine(phase, 1)
        advance(factor, 8)
        settle(phase + 1, 1)
        share(phase + 1, 1)
        advance(factor, 100)
    factor_copy(0, c).start()

    for half in range(2):
        shared(2, half)
    factor_copy(0, 1 - c).wait_recv()
    for half in range(2):
        half_copy(2, half, 1 - c).wait_recv()

    def normalise(i, _):
        rows = part(i, 256)
        for s in range(2):
            lanes = slice(s * H, s * H + H)
            product = jnp.concatenate([bs[2, 0, rows, lanes], bs[2, 1, rows, lanes]], 1)
            new = dot_full(product, linv[0, s], NT)
            zb[0, rows, lanes] = new[:, 0:H]
            zb[1, rows, lanes] = new[:, H:K]
        return 0

    lax.fori_loop(0, 2, normalise, 0)

    squares(2, zb.at[0], zb.at[1])
    for half in range(2):
        high, low = split(zb[half])
        bh[half] = high
        bl[half] = low

    def chunks(r, _):
        rows = part(r, 128)
        for half in range(2):
            both = dot3(xth[rows, :], xtl[rows, :], bh[half], bl[half])
            own[2, 4 * half + r] = jnp.where(slot_of(4 * c + r) == 0, both[:, 0:H], both[:, H:K])
            send_own(2, 4 * half + r)
        return 0

    lax.fori_loop(0, 4, chunks, 0)
    order = [8, 9, 10, 0, 4, 1, 5, 2, 6, 3, 7]
    relay(2, order[0:2], [], [])
    relay(2, order[2:3], [], [])
    relay(2, order[3:4], order[0:1], order[0:3])
    factor = inverse_factor(tot.at[2, 8], tot.at[2, 9], tot.at[2, 10], linv.at[1, c])
    for step in range(4, 11):
        advance(factor, 4 if step > 5 else 2)
        relay(2, order[step : step + 1], order[step - 3 : step - 2], [])
    for step in range(8, 11):
        advance(factor, 3)
        relay(2, [], order[step : step + 1], [])
    advance(factor, 100)
    factor_copy(1, c).start()

    def deliver(row):
        relay(2, [], [], [row, 4 + row])
        y3[4 * c + row] = jnp.concatenate([tot[2, row], tot[2, 4 + row]], 1)
        y_copy(row, c).start()

    for row in range(3):
        deliver(row)
    factor_copy(1, 1 - c).wait_recv()
    for s in range(2):
        lanes = slice(s * H, s * H + H)
        vectors = jnp.concatenate([zb[0, part(c, 256), lanes], zb[1, part(c, 256), lanes]], 1)
        high, low = split(dot_full(vectors, linv[1, s], NT))
        bh[s, 0:256, :] = high
        bl[s, 0:256, :] = low
        high, low = split(linv[1, s])
        bh[s, 256:512, :] = high
        bl[s, 256:512, :] = low

    def out_copy(r):
        columns = part(r, 128)
        return pltpu.make_async_copy(found.at[:, columns], out.at[:, columns], local.at[r])

    def clean(r):
        s = slot_of(r)
        high, low = split(y3[r])
        coefficients = dot3(high, low, bh[s, 256:512, :], bl[s, 256:512, :], NT)
        high, low = split(coefficients)
        found[:, part(r, 128)] = dot3(bh[s, 0:256, :], bl[s, 0:256, :], high, low, NT)
        out_copy(r).start()

    def clean_both(row, _):
        clean(4 * c + row)
        y_copy(row, 1 - c).wait_recv()
        clean(4 * (1 - c) + row)
        return 0

    lax.fori_loop(0, 3, clean_both, 0)
    deliver(3)
    clean_both(3, 0)

    for r in range(8):
        out_copy(r).wait()
    x_copy().wait_send()
    base_copy(zh).wait_send()
    each_peer(lambda d: id_copy(d, q).wait_send())
    for row in range(4):
        y_copy(row, c).wait_send()
    for half in range(2):
        factor_copy(half, c).wait_send()
        for phase in range(3):
            each_peer(lambda d: g_copy(phase, half, d, q).wait_send())
            half_copy(phase, half, c).wait_send()
        for phase in range(2):
            each_peer(lambda d: r_copy(phase, half, d, q).wait_send())
            p_copy(phase, half).wait_send()
    for phase in range(3):
        count = 11 if phase > 0 else 8

        @pl.when(is_mid)
        def _():
            def sent(ch, _):
                mid_copy(phase, ch).wait_send()
                total_copy(phase, ch).wait_send()
                return 0

            lax.fori_loop(0, count, sent, 0)

        @pl.when(is_end)
        def _():
            def sent(ch, _):
                end_copy(phase, ch).wait_send()
                return 0

            lax.fori_loop(0, count, sent, 0)


def solution(mesh):
    def step(frames, ann_rows, start_bases):
        anywhere = pl.BlockSpec(memory_space=pl.ANY)
        dma = pltpu.SemaphoreType.DMA
        found = pl.pallas_call(
            kernel,
            out_shape=jax.ShapeDtypeStruct(frames.shape, F32),
            in_specs=[pl.BlockSpec(memory_space=pltpu.HBM), pl.BlockSpec(memory_space=pltpu.SMEM), pl.BlockSpec(memory_space=pltpu.HBM)],
            out_specs=anywhere,
            scratch_shapes=[
                pltpu.VMEM((256, 1024), F32),
                pltpu.VMEM((ANN, 8, K), F32),
                pltpu.VMEM((256, 512), F32),
                pltpu.VMEM((512, 512), BF16),
                pltpu.VMEM((512, 512), BF16),
                pltpu.VMEM((512, 512), BF16),
                pltpu.VMEM((512, 512), BF16),
                pltpu.VMEM((3, 2, 512, K), F32),
                pltpu.VMEM((2, 512, K), BF16),
                pltpu.VMEM((2, 512, K), BF16),
                pltpu.VMEM((2, 512, K), F32),
                pltpu.VMEM((3, CHUNKS, 128, H), F32),
                pltpu.VMEM((3, CHUNKS, 128, H), F32),
                pltpu.VMEM((3, CHUNKS, 128, H), F32),
                pltpu.VMEM((3, CHUNKS, 128, H), F32),
                pltpu.VMEM((2, 512, K), BF16),
                pltpu.VMEM((2, 512, K), BF16),
                pltpu.VMEM((2, 2, 512, K), F32),
                pltpu.VMEM((2, 2, 256, K), F32),
                pltpu.VMEM((2, 2, 256, K), F32),
                pltpu.VMEM((2, 2, NPL, 16, K), F32),
                pltpu.VMEM((3, 2, ANN, 16, H), F32),
                pltpu.VMEM((2, 2, ANN, 16, H), F32),
                pltpu.VMEM((3, 2, NPL, 16, K), F32),
                pltpu.VMEM((8, K), jnp.int32),
                pltpu.VMEM((NPL, 8, K), jnp.int32),
                pltpu.VMEM((2, 2, K, K), F32),
                pltpu.VMEM((8, 128, K), F32),
                pltpu.VMEM((2, ANN, 8, H), F32),
                pltpu.VMEM((256, 1024), F32),
                dma((10,)),
                dma((17,)), dma((17,)),
                dma((11, NPL)), dma((11, NPL)),
                dma((5,)), dma((5,)),
                dma((3, 3, CHUNKS)), dma((3, 3, CHUNKS)),
            ],
            compiler_params=pltpu.CompilerParams(
                collective_id=0, has_side_effects=True, vmem_limit_bytes=52 * 1024 * 1024
            ),
        )(frames, ann_rows, start_bases)
        return frames - found

    return jax.shard_map(
        step,
        mesh=mesh,
        in_specs=(P("tm", "pix"), P("pix"), P(None, ("tm", "pix"), None)),
        out_specs=P("tm", "pix"),
        check_vma=False,
    )
```
